32 devices in a mesh: role: 2 (over core), slab: 16 (over z, y, x).
Axes of the slice: x: 2, y: 2, z: 4, core: 2. Of those that a mesh axis runs over, the one named last changes fastest.
Arguments:
- velocity: float32 [4, 32, 128, 256], P(None, 'slab', 'role'), may hold values from -18 to 18
- basis: bfloat16 [256, 32, 128, 256], P(None, 'slab', 'role'), may hold values from -1 to 1, as said below
- mean_flow: float32 [128], replicated, may hold values from 0.2 to 2
- shear: float32 [128], replicated, may hold values from -1 to 1
Outputs:
- advanced: float32 [4, 32, 128, 256], P(None, 'slab', 'role')
- coeffs: float32 [256, 8], replicated
- rfactor: float32 [8, 8], replicated
- directions: float32 [8, 32, 128, 256], P(None, 'slab', 'role')
The draws below stay inside these ranges and needn't reach their ends.
Inputs may be any that keep to these rules, and one draw needn't show every extreme that they name: Every column of the basis has length within a few percent of one, and distinct columns are nearly orthogonal.
All inputs are finite; a program needn't handle non-finite values.
Results may differ from the reference program's by a relative error of at most 0.00035.
The reference program's roundings to bfloat16 on the way count: a program that leaves them out, or rounds other values in their place, can miss the bound.
Values sent between devices are 32-bit elements; how exact they have to be, the bound alone decides.
A program may use at most 128 MiB of HBM per device.

```python
import math
import jax
import jax.numpy as jnp
from jax import lax

NZ = 256
NQ = 4
K = 256
NX = 32
NY = 128


def column_values(key, column_index):
    column_key = jax.random.fold_in(jax.random.fold_in(key, 7001), column_index)
    return jax.random.truncated_normal(column_key, -4.0, 4.0, (NX, NY, NZ), jnp.float32)


def draw_basis(key, part):
    column_scale = 1.0 / math.sqrt(NX * NY * NZ)
    return lax.map(lambda column_index: column_values(key, column_index) * column_scale, jnp.arange(K, dtype=jnp.int32)).astype(jnp.bfloat16)


def draw_velocity(key, part):
    picked = jax.random.permutation(jax.random.fold_in(key, 7002), K)[:NQ * 8].reshape(NQ, 8)
    sign_values = (jax.random.randint(jax.random.fold_in(key, 7003), (NQ, 8), 0, 2) * 2 - 1).astype(jnp.float32)
    weights = sign_values * jax.random.uniform(jax.random.fold_in(key, 7004), (NQ, 8), jnp.float32, 0.25, 0.5)
    noise_key = jax.random.fold_in(key, 7005)
    noise_part = 0.5 * jax.random.truncated_normal(noise_key, -4.0, 4.0, (NQ, NX, NY, NZ), jnp.float32)
    fields = []
    for field_index in range(NQ):
        running = noise_part[field_index]
        for term_index in range(8):
            running = running + weights[field_index, term_index] * column_values(key, picked[field_index, term_index])
        fields.append(running)
    return jnp.stack(fields)


def setup_inputs(seed: int = 0) -> dict:
    seeds = jax.random.split(jax.random.key(seed), 5)
    velocity = draw_velocity(jax.random.fold_in(seeds[4], 71), 0)
    basis = draw_basis(jax.random.fold_in(seeds[4], 71), 0)
    mean_flow = jnp.clip(jnp.exp(jax.random.uniform(seeds[2], (NY,), jnp.float32, math.log(0.2), math.log(2.0))), 0.2, 2.0)
    shear = jnp.clip(jax.random.uniform(seeds[3], (NY,), jnp.float32, -1.0, 1.0), -1.0, 1.0)
    return dict(velocity=velocity, basis=basis, mean_flow=mean_flow, shear=shear)


viscosity = 0.1
time_step = 0.4

def offset_slice(padded, offset, dimension, length):
    return lax.slice_in_dim(padded, 2 + offset, 2 + offset + length, axis=dimension)

def second_diff(padded, center, dimension, length):
    return (-offset_slice(padded, 2, dimension, length) + 16.0 * offset_slice(padded, 1, dimension, length) - 30.0 * center + 16.0 * offset_slice(padded, -1, dimension, length) - offset_slice(padded, -2, dimension, length)) / 12.0

def tendency(center, xpadded, ypadded, mean_flow, shear):
    nx_loc = center.shape[1]
    ny_loc = center.shape[2]
    nz_loc = center.shape[3]
    zpadded = jnp.concatenate([center[..., -2:], center, center[..., :2]], axis=3)
    first_x = (-offset_slice(xpadded, 2, 1, nx_loc) + 8.0 * offset_slice(xpadded, 1, 1, nx_loc) - 8.0 * offset_slice(xpadded, -1, 1, nx_loc) + offset_slice(xpadded, -2, 1, nx_loc)) / 12.0
    laplace = second_diff(xpadded, center, 1, nx_loc) + second_diff(ypadded, center, 2, ny_loc) + second_diff(zpadded, center, 3, nz_loc)
    profile = mean_flow[None, None, :, None]
    result = -profile * first_x + viscosity * laplace
    shear_term = shear[None, None, :, None] * center[1:2]
    return jnp.concatenate([result[:1] - shear_term, result[1:]], axis=0)

def full_tendency(state, mean_flow, shear):
    xpadded = jnp.pad(state, ((0, 0), (2, 2), (0, 0), (0, 0)), mode='wrap')
    ypadded = jnp.pad(state, ((0, 0), (0, 0), (2, 2), (0, 0)))
    return tendency(state, xpadded, ypadded, mean_flow, shear)

def reference(velocity, basis, mean_flow, shear):
    tend_zero = full_tendency(velocity, mean_flow, shear)
    segment_one = velocity + time_step * (8.0 / 15.0) * tend_zero
    tend_one = full_tendency(segment_one, mean_flow, shear)
    advanced = segment_one + time_step * (5.0 / 12.0 * tend_one - 17.0 / 60.0 * tend_zero)
    snapshots = jnp.concatenate([segment_one, advanced], axis=0)
    flat_snaps = snapshots.reshape(snapshots.shape[0], -1)
    snaps_bf = flat_snaps.astype(jnp.bfloat16)
    basis_rows = basis.reshape(basis.shape[0], -1)
    coeffs = jnp.dot(basis_rows.astype(jnp.float32), snaps_bf.T.astype(jnp.float32), preferred_element_type=jnp.float32)
    coeffs_bf = coeffs.astype(jnp.bfloat16)
    residual = flat_snaps - jnp.dot(coeffs_bf.T.astype(jnp.float32), basis_rows.astype(jnp.float32), preferred_element_type=jnp.float32)
    gram_matrix = jnp.dot(residual, residual.T, precision=lax.Precision.HIGHEST)
    lower_factor = jnp.linalg.cholesky(gram_matrix)
    directions = jax.scipy.linalg.solve_triangular(lower_factor, residual, lower=True)
    return (advanced, coeffs, lower_factor.T, directions.reshape(snapshots.shape))
```

```python
import functools

import jax
import jax.numpy as jnp
from jax import lax
from jax.experimental import pallas as pl
from jax.experimental.pallas import tpu as pltpu
from jax.sharding import PartitionSpec as P

viscosity = 0.1
time_step = 0.4
MESH = pl.DeviceIdType.MESH
HIGHEST = lax.Precision.HIGHEST
T = 16


def iota(shape, dim):
    return lax.broadcasted_iota(jnp.int32, shape, dim)


def same_row(rows, cols):
    return (iota((rows, cols), 0) % T) == (iota((rows, cols), 1) % T)


def nt_dot(a, b, precision=None):
    return lax.dot_general(
        a, b, (((1,), (1,)), ((), ())), precision=precision, preferred_element_type=jnp.float32
    )


def kernel(groups, v_ref, basis_ref, flow_ref, shear_ref,
           adv_ref, coef_ref, r_ref, dir_ref,
           bas, s1, halo, yh, yx, prof, tend, sbf, racc, cbig, wres,
           pa, pb, ga, gb,
           bas_sem, part_s, part_r, fwd_s, fwd_r, z_s, z_r, y_s, y_r,
           pa_s, pa_r, pb_s, pb_r, ga_s, ga_r, gb_s, gb_r):
    nf, nx, ny, nz = v_ref.shape
    nk = bas.shape[0]
    nyg = ny // T
    cells = nx * nyg
    role = lax.axis_index("role")
    slab = lax.axis_index("slab")
    j = slab % 4
    g = slab // 4
    base = g * 4
    partner = base + j + 1 - 2 * (j % 2)
    across = base + (j + 2) % 4
    zto = ((g + 1 - 2 * (j // 2) + groups) % groups) * 4 + j
    lslot = (1 - j % 2) * (2 - j // 2)
    rslot = (j % 2) * (1 + j // 2)
    me8 = role * 4 + j

    basis_copy = pltpu.make_async_copy(basis_ref, bas, bas_sem)
    basis_copy.start()

    barrier = pltpu.get_barrier_semaphore()
    plane_peers = []
    for o in range(1, 8):
        p = (me8 + o) % 8
        plane_peers.append((p, (p // 4, base + p % 4)))
    group_peers = []
    for o in range(1, groups):
        p = (g + o) % groups
        group_peers.append((p, (role, p * 4 + j)))
    for _, dev in plane_peers + group_peers:
        pl.semaphore_signal(barrier, inc=1, device_id=dev, device_id_type=MESH)
    pl.semaphore_wait(barrier, 6 + groups)

    def remote(src, dst, ss, rs, dev):
        return pltpu.make_async_remote_copy(
            src_ref=src, dst_ref=dst, send_sem=ss, recv_sem=rs, device_id=dev, device_id_type=MESH
        )

    chunks = 2 * nf * nx

    def where_of(c):
        e, rest = divmod(c, nf * nx)
        return e, rest // nx, rest % nx

    def part_copy(c):
        e, f, x = where_of(c)
        src = (v_ref if e == 0 else s1).at[f, x]
        return remote(src, halo.at[e, 0, f, x], part_s.at[c], part_r.at[c], (role, partner))

    def fwd_copy(c):
        e, f, x = where_of(c)
        return remote(halo.at[e, 0, f, x], halo.at[e, 1, f, x], fwd_s.at[c], fwd_r.at[c], (role, across))

    def z_copy(c):
        e, f, x = where_of(c)
        return remote(halo.at[e, 1, f, x], halo.at[e, 2, f, x], z_s.at[c], z_r.at[c], (role, zto))

    row0 = pl.multiple_of((1 - role) * (ny - 8), 8)

    def y_copy(e, f):
        src = (v_ref if e == 0 else s1).at[f, :, pl.ds(row0, 8), :]
        i = e * nf + f
        return remote(src, yh.at[e, f], y_s.at[i], y_r.at[i], (1 - role, slab))

    for c in range(nf * nx):
        part_copy(c).start()
    for f in range(nf):
        y_copy(0, f).start()

    total = flow_ref.shape[1]
    pick = iota((ny, total), 1) == iota((ny, total), 0) + role * ny
    for i, ref in enumerate((flow_ref, shear_ref)):
        col = jnp.sum(jnp.where(pick, ref[...], 0.0), axis=1, keepdims=True)
        prof[i] = jnp.broadcast_to(col, (ny, nz))
    role_f = role.astype(jnp.float32)

    def tendency(e, f):
        src = v_ref if e == 0 else s1
        layers = [halo[e, lslot, f, 0], halo[e, lslot, f, 1], src[f, 0], src[f, 1],
                  halo[e, rslot, f, 0], halo[e, rslot, f, 1]]
        out = []
        for x in range(nx):
            l2, l1, q, r1, r2 = layers[x:x + 5]
            edge = yh[e, f, x]
            yx[x, 0:8, :] = edge * role_f
            yx[x, 8:8 + ny, :] = q
            yx[x, 8 + ny:16 + ny, :] = edge * (1.0 - role_f)
            near = (l1 + r1) + (yx[x, 7:7 + ny, :] + yx[x, 9:9 + ny, :])
            far = (l2 + r2) + (yx[x, 6:6 + ny, :] + yx[x, 10:10 + ny, :])
            near = near + (pltpu.roll(q, 1, 1) + pltpu.roll(q, nz - 1, 1))
            far = far + (pltpu.roll(q, 2, 1) + pltpu.roll(q, nz - 2, 1))
            first = (8.0 * (r1 - l1) - (r2 - l2)) * (1.0 / 12.0)
            lap = (16.0 * near - far - 90.0 * q) * (viscosity / 12.0)
            res = lap - prof[0] * first
            if f == 0:
                res = res - prof[1] * src[1, x]
            out.append(res)
        return out

    def keep_rounded(half, f, x, vals):
        for yg in range(nyg):
            sbf[half, x * nyg + yg, f * T:(f + 1) * T, :] = vals[yg * T:(yg + 1) * T, :].astype(jnp.bfloat16)

    def project(half, kb):
        acc = None
        for i in range(cells):
            x, y0 = i // nyg, (i % nyg) * T
            lhs = bas[pl.ds(kb * T, T), x, y0:y0 + T, :].reshape(T * T, nz)
            d = nt_dot(lhs, sbf[half, i])
            acc = d if acc is None else acc + d
        acc = jnp.where(same_row(T * T, nf * T), acc, 0.0)
        racc[half, pl.ds(pl.multiple_of(kb * T, T), T), :] = jnp.sum(acc.reshape(T, T, nf * T), axis=1)

    def project_range(half, lo, hi):
        def body(kb, carry):
            project(half, kb)
            return carry
        lax.fori_loop(lo, hi, body, 0)

    nkb = nk // T
    edge_chip = j % 3 == 0
    done_kb = 0
    for t in range(chunks + 2):
        if t < chunks:
            part_copy(t).wait_recv()
            fwd_copy(t).start()
        if 0 <= t - 1 < chunks:
            fwd_copy(t - 1).wait_recv()

            @pl.when(edge_chip)
            def _():
                z_copy(t - 1).start()
        if t - 2 >= 0:
            c = t - 2

            @pl.when(edge_chip)
            def _():
                z_copy(c).wait_recv()
            e, f, x = where_of(c)
            if x == nx - 1:
                y_copy(e, f).wait_recv()
                tens = tendency(e, f)
                if e == 0:
                    for xx in range(nx):
                        val = v_ref[f, xx] + (time_step * 8.0 / 15.0) * tens[xx]
                        s1[f, xx] = val
                        tend[f, xx] = tens[xx]
                        keep_rounded(0, f, xx, val)
                    for xx in range(nx):
                        part_copy(nf * nx + f * nx + xx).start()
                    y_copy(1, f).start()
                else:
                    for xx in range(nx):
                        val = s1[f, xx] + (
                            (time_step * 5.0 / 12.0) * tens[xx] - (time_step * 17.0 / 60.0) * tend[f, xx]
                        )
                        adv_ref[f, xx] = val
                        keep_rounded(1, f, xx, val)
        first = nf * nx + 2
        if t >= first:
            if t == first:
                basis_copy.wait()
            upto = ((t - first + 1) * nkb) // (chunks + 2 - first)
            project_range(0, done_kb, upto)
            done_kb = upto
    project_range(1, 0, nkb)

    pt = None
    for half in range(2):
        pick8 = (iota((8, nf * T), 0) - nf * half == iota((8, nf * T), 1) // T).astype(jnp.float32)
        d = nt_dot(pick8, racc[half], HIGHEST)
        pt = d if pt is None else pt + d

    def all_sum(val, a, b, a_s, a_r, b_s, b_r):
        a[me8] = val
        for p, dev in plane_peers:
            remote(a.at[me8], a.at[me8], a_s.at[p], a_r.at[me8], dev).start()
        for p, dev in plane_peers:
            remote(a.at[p], a.at[p], a_s.at[p], a_r.at[p], dev).wait_recv()
        val = a[0]
        for i in range(1, 8):
            val = val + a[i]
        b[g] = val
        for p, dev in group_peers:
            remote(b.at[g], b.at[g], b_s.at[p], b_r.at[g], dev).start()
        for p, dev in group_peers:
            remote(b.at[p], b.at[p], b_s.at[p], b_r.at[p], dev).wait_recv()
        val = b[0]
        for i in range(1, groups):
            val = val + b[i]
        return val

    def all_sum_sent(a, b, a_s, a_r, b_s, b_r):
        for p, dev in plane_peers:
            remote(a.at[me8], a.at[me8], a_s.at[p], a_r.at[me8], dev).wait_send()
        for p, dev in group_peers:
            remote(b.at[g], b.at[g], b_s.at[p], b_r.at[g], dev).wait_send()

    coeffs = all_sum(pt, pa, pb, pa_s, pa_r, pb_s, pb_r)
    coef_ref[...] = coeffs
    cb = coeffs.astype(jnp.bfloat16)

    ns = 2 * nf

    def spread(kb, carry):
        rep = (iota((nk, T * T), 0) == kb * T + iota((nk, T * T), 1) // T)
        rep = rep.astype(jnp.float32).astype(jnp.bfloat16)
        row = jnp.dot(cb, rep, preferred_element_type=jnp.float32)
        full = jnp.broadcast_to(row[:, None, :], (ns, T, T * T)).reshape(ns * T, T * T)
        cbig[kb] = jnp.where(same_row(ns * T, T * T), full, 0.0).astype(jnp.bfloat16)
        return carry

    lax.fori_loop(0, nkb, spread, 0)

    def residual(i, gram):
        x = i // nyg
        y0 = pl.multiple_of((i % nyg) * T, T)
        acc = None
        for kb in range(nkb):
            rhs = bas[kb * T:(kb + 1) * T, x, pl.ds(y0, T), :].reshape(T * T, nz)
            d = jnp.dot(cbig[kb], rhs, preferred_element_type=jnp.float32)
            acc = d if acc is None else acc + d
        snap = jnp.concatenate(
            [s1[:, x, pl.ds(y0, T), :].reshape(nf * T, nz), adv_ref[:, x, pl.ds(y0, T), :].reshape(nf * T, nz)],
            axis=0,
        )
        w = snap - acc
        wres[i] = w
        return gram + nt_dot(w, w, HIGHEST)

    gram = lax.fori_loop(0, cells, residual, jnp.zeros((ns * T, ns * T), jnp.float32))
    gram = jnp.where(same_row(ns * T, ns * T), gram, 0.0)
    gram = jnp.sum(gram.reshape(ns, T, ns * T), axis=1)
    gram = all_sum(gram, ga, gb, ga_s, ga_r, gb_s, gb_r)

    wide = ns * T
    fold = (iota((wide, wide), 0) // T == iota((wide, wide), 1)).astype(jnp.float32)
    rows, cols = iota((ns, wide), 0), iota((ns, wide), 1)
    aug = jnp.dot(gram, fold, precision=HIGHEST, preferred_element_type=jnp.float32)
    aug = jnp.where(cols == rows + ns, 1.0, aug)
    for p in range(ns):
        col = jnp.broadcast_to(aug[:, p:p + 1], (ns, wide))
        inv = 1.0 / jnp.sqrt(jnp.broadcast_to(col[p:p + 1, :], (ns, wide)))
        top = jnp.broadcast_to(aug[p:p + 1, :], (ns, wide)) * inv
        aug = jnp.where(rows == p, top, jnp.where(rows > p, aug - (col * inv) * top, aug))
    r_ref[...] = jnp.where(cols >= rows, aug, 0.0)[:, :ns]

    unfold = (iota((wide, wide), 0) == ns + iota((wide, wide), 1) // T).astype(jnp.float32)
    mix = jnp.dot(aug, unfold, precision=HIGHEST, preferred_element_type=jnp.float32)
    mix = jnp.broadcast_to(mix[:, None, :], (ns, T, wide)).reshape(wide, wide)
    mix = jnp.where(same_row(wide, wide), mix, 0.0)

    def solve(i, carry):
        x = i // nyg
        y0 = pl.multiple_of((i % nyg) * T, T)
        d = jnp.dot(mix, wres[i], precision=HIGHEST, preferred_element_type=jnp.float32)
        dir_ref[:, x, pl.ds(y0, T), :] = d.reshape(ns, T, nz)
        return carry

    lax.fori_loop(0, cells, solve, 0)

    for c in range(chunks):
        part_copy(c).wait_send()
        fwd_copy(c).wait_send()
    for e in range(2):
        for f in range(nf):
            y_copy(e, f).wait_send()

    @pl.when(edge_chip)
    def _():
        for c in range(chunks):
            z_copy(c).wait_send()
    all_sum_sent(pa, pb, pa_s, pa_r, pb_s, pb_r)
    all_sum_sent(ga, gb, ga_s, ga_r, gb_s, gb_r)


def on_device(velocity, basis, mean_flow, shear):
    nf, nx, ny, nz = velocity.shape
    nk = basis.shape[0]
    groups = lax.axis_size("slab") // 4
    ns = 2 * nf
    cells = nx * ny // T
    f32, bf16 = jnp.float32, jnp.bfloat16
    chunks = 2 * nf * nx
    dma = pltpu.SemaphoreType.DMA
    vmem = pl.BlockSpec(memory_space=pltpu.VMEM)
    scratch = [
        pltpu.VMEM((nk, nx, ny, nz), bf16),
        pltpu.VMEM((nf, nx, ny, nz), f32),
        pltpu.VMEM((2, 3, nf, nx, ny, nz), f32),
        pltpu.VMEM((2, nf, nx, 8, nz), f32),
        pltpu.VMEM((nx, ny + 16, nz), f32),
        pltpu.VMEM((2, ny, nz), f32),
        pltpu.VMEM((nf, nx, ny, nz), f32),
        pltpu.VMEM((2, cells, nf * T, nz), bf16),
        pltpu.VMEM((2, nk, nf * T), f32),
        pltpu.VMEM((nk // T, ns * T, T * T), bf16),
        pltpu.VMEM((cells, ns * T, nz), f32),
        pltpu.VMEM((8, ns, nk), f32),
        pltpu.VMEM((groups, ns, nk), f32),
        pltpu.VMEM((8, ns, ns * T), f32),
        pltpu.VMEM((groups, ns, ns * T), f32),
        dma,
        *([dma((chunks,))] * 6),
        *([dma((2 * nf,))] * 2),
        *([dma((8,))] * 2),
        *([dma((groups,))] * 2),
        *([dma((8,))] * 2),
        *([dma((groups,))] * 2),
    ]
    advanced, coeffs, rfactor, directions = pl.pallas_call(
        functools.partial(kernel, groups),
        out_shape=[
            jax.ShapeDtypeStruct((nf, nx, ny, nz), f32),
            jax.ShapeDtypeStruct((ns, nk), f32),
            jax.ShapeDtypeStruct((ns, ns), f32),
            jax.ShapeDtypeStruct((ns, nx, ny, nz), f32),
        ],
        in_specs=[vmem, pl.BlockSpec(memory_space=pl.ANY), vmem, vmem],
        out_specs=[vmem] * 4,
        scratch_shapes=scratch,
        compiler_params=pltpu.CompilerParams(
            collective_id=0, has_side_effects=True, vmem_limit_bytes=48 * 1024 * 1024
        ),
    )(velocity, basis, mean_flow.reshape(1, -1), shear.reshape(1, -1))
    return advanced, coeffs.T, rfactor, directions


def solution(mesh):
    return jax.shard_map(
        on_device,
        mesh=mesh,
        in_specs=(P(None, "slab", "role", None), P(None, "slab", "role", None), P(), P()),
        out_specs=(P(None, "slab", "role", None), P(), P(), P(None, "slab", "role", None)),
        check_vma=False,
    )
```

```python
import functools

import jax
import jax.numpy as jnp
from jax import lax
from jax.experimental import pallas as pl
from jax.experimental.pallas import tpu as pltpu
from jax.sharding import PartitionSpec as P

viscosity = 0.1
time_step = 0.4
MESH = pl.DeviceIdType.MESH
HIGHEST = lax.Precision.HIGHEST
T = 16


def iota(shape, dim):
    return lax.broadcasted_iota(jnp.int32, shape, dim)


def same_row(rows, cols):
    return (iota((rows, cols), 0) % T) == (iota((rows, cols), 1) % T)


def nt_dot(a, b, precision=None):
    return lax.dot_general(
        a, b, (((1,), (1,)), ((), ())), precision=precision, preferred_element_type=jnp.float32
    )


def kernel(groups, v_hbm, basis_ref, flow_hbm, shear_hbm,
           adv_ref, coef_ref, r_ref, dir_ref,
           v_ref, flow_ref, shear_ref, rep16,
           bas, s1, halo, yh, yx, prof, tend, sbf, racc, cbig, wres,
           pa, pb, ga, gb,
           in_sem, bas_sem, part_s, part_r, fwd_s, fwd_r, z_s, z_r, y_s, y_r,
           pa_s, pa_r, pb_s, pb_r, ga_s, ga_r, gb_s, gb_r):
    nf, nx, ny, nz = v_ref.shape
    nk = bas.shape[0]
    nyg = ny // T
    cells = nx * nyg
    role = lax.axis_index("role")
    slab = lax.axis_index("slab")
    j = slab % 4
    g = slab // 4
    base = g * 4
    partner = base + j + 1 - 2 * (j % 2)
    across = base + (j + 2) % 4
    zto = ((g + 1 - 2 * (j // 2) + groups) % groups) * 4 + j
    lslot = (1 - j % 2) * (2 - j // 2)
    rslot = (j % 2) * (1 + j // 2)
    me8 = role * 4 + j

    small = [(v_hbm, v_ref), (flow_hbm, flow_ref), (shear_hbm, shear_ref)]
    loads = [pltpu.make_async_copy(src, dst, in_sem.at[i]) for i, (src, dst) in enumerate(small)]
    for load in loads:
        load.start()
    basis_copy = pltpu.make_async_copy(basis_ref, bas, bas_sem)
    basis_copy.start()

    barrier = pltpu.get_barrier_semaphore()
    plane_peers = []
    for o in range(1, 8):
        p = (me8 + o) % 8
        plane_peers.append((p, (p // 4, base + p % 4)))
    group_peers = []
    for o in range(1, groups):
        p = (g + o) % groups
        group_peers.append((p, (role, p * 4 + j)))
    for _, dev in plane_peers + group_peers:
        pl.semaphore_signal(barrier, inc=1, device_id=dev, device_id_type=MESH)
    for load in loads:
        load.wait()
    pl.semaphore_wait(barrier, 6 + groups)

    def remote(src, dst, ss, rs, dev):
        return pltpu.make_async_remote_copy(
            src_ref=src, dst_ref=dst, send_sem=ss, recv_sem=rs, device_id=dev, device_id_type=MESH
        )

    chunks = 2 * nf * nx
    window, fwd_lag, z_lag = 4, 2, 4

    def where_of(c):
        e, rest = divmod(c, nf * nx)
        return e, rest // nx, rest % nx

    def part_copy(c):
        e, f, x = where_of(c)
        src = (v_ref if e == 0 else s1).at[f, x]
        return remote(src, halo.at[e, 0, f, x], part_s.at[c], part_r.at[c], (role, partner))

    def fwd_copy(c):
        e, f, x = where_of(c)
        return remote(halo.at[e, 0, f, x], halo.at[e, 1, f, x], fwd_s.at[c], fwd_r.at[c], (role, across))

    def z_copy(c):
        e, f, x = where_of(c)
        return remote(halo.at[e, 1, f, x], halo.at[e, 2, f, x], z_s.at[c], z_r.at[c], (role, zto))

    row0 = pl.multiple_of((1 - role) * (ny - 8), 8)

    def y_copy(e, f):
        src = (v_ref if e == 0 else s1).at[f, :, pl.ds(row0, 8), :]
        i = e * nf + f
        return remote(src, yh.at[e, f], y_s.at[i], y_r.at[i], (1 - role, slab))

    for c in range(window):
        part_copy(c).start()
    for f in range(nf):
        y_copy(0, f).start()

    total = flow_ref.shape[1]
    pick = iota((ny, total), 1) == iota((ny, total), 0) + role * ny
    for i, ref in enumerate((flow_ref, shear_ref)):
        col = jnp.sum(jnp.where(pick, ref[...], 0.0), axis=1, keepdims=True)
        prof[i] = jnp.broadcast_to(col, (ny, nz))
    spot = iota((nk, T * T), 0) % T == iota((nk, T * T), 1) // T
    rep16[...] = spot.astype(jnp.float32).astype(jnp.bfloat16)
    role_f = role.astype(jnp.float32)

    def tendency(e, f):
        src = v_ref if e == 0 else s1
        layers = [halo[e, lslot, f, 0], halo[e, lslot, f, 1], src[f, 0], src[f, 1],
                  halo[e, rslot, f, 0], halo[e, rslot, f, 1]]
        out = []
        for x in range(nx):
            l2, l1, q, r1, r2 = layers[x:x + 5]
            edge = yh[e, f, x]
            yx[x, 0:8, :] = edge * role_f
            yx[x, 8:8 + ny, :] = q
            yx[x, 8 + ny:16 + ny, :] = edge * (1.0 - role_f)
            near = (l1 + r1) + (yx[x, 7:7 + ny, :] + yx[x, 9:9 + ny, :])
            far = (l2 + r2) + (yx[x, 6:6 + ny, :] + yx[x, 10:10 + ny, :])
            near = near + (pltpu.roll(q, 1, 1) + pltpu.roll(q, nz - 1, 1))
            far = far + (pltpu.roll(q, 2, 1) + pltpu.roll(q, nz - 2, 1))
            first = (8.0 * (r1 - l1) - (r2 - l2)) * (1.0 / 12.0)
            lap = (16.0 * near - far - 90.0 * q) * (viscosity / 12.0)
            res = lap - prof[0] * first
            if f == 0:
                res = res - prof[1] * src[1, x]
            out.append(res)
        return out

    def keep_rounded(half, f, x, vals):
        for yg in range(nyg):
            sbf[half, x * nyg + yg, f * T:(f + 1) * T, :] = vals[yg * T:(yg + 1) * T, :].astype(jnp.bfloat16)

    def project(half, kb):
        acc = None
        for i in range(cells):
            x, y0 = i // nyg, (i % nyg) * T
            lhs = bas[pl.ds(kb * T, T), x, y0:y0 + T, :].reshape(T * T, nz)
            d = nt_dot(lhs, sbf[half, i])
            acc = d if acc is None else acc + d
        acc = jnp.where(same_row(T * T, nf * T), acc, 0.0)
        racc[half, pl.ds(pl.multiple_of(kb * T, T), T), :] = jnp.sum(acc.reshape(T, T, nf * T), axis=1)

    def project_range(half, lo, hi):
        def body(kb, carry):
            project(half, kb)
            return carry
        lax.fori_loop(lo, hi, body, 0, unroll=2)

    nkb = nk // T
    edge_chip = j % 3 == 0
    done_kb = 0
    for t in range(chunks + z_lag):
        if t < chunks:
            part_copy(t).wait_recv()
            fwd_copy(t).start()
            if t + window < nf * nx:
                part_copy(t + window).start()
        if 0 <= t - fwd_lag < chunks:
            fwd_copy(t - fwd_lag).wait_recv()

            @pl.when(edge_chip)
            def _():
                z_copy(t - fwd_lag).start()
        if t - z_lag >= 0:
            c = t - z_lag

            @pl.when(edge_chip)
            def _():
                z_copy(c).wait_recv()
            e, f, x = where_of(c)
            if x == nx - 1:
                y_copy(e, f).wait_recv()
                tens = tendency(e, f)
                if e == 0:
                    for xx in range(nx):
                        val = v_ref[f, xx] + (time_step * 8.0 / 15.0) * tens[xx]
                        s1[f, xx] = val
                        tend[f, xx] = tens[xx]
                        keep_rounded(0, f, xx, val)
                    for xx in range(nx):
                        part_copy(nf * nx + f * nx + xx).start()
                    y_copy(1, f).start()
                else:
                    for xx in range(nx):
                        val = s1[f, xx] + (
                            (time_step * 5.0 / 12.0) * tens[xx] - (time_step * 17.0 / 60.0) * tend[f, xx]
                        )
                        adv_ref[f, xx] = val
                        keep_rounded(1, f, xx, val)
        first = nf * nx + z_lag
        if t >= first:
            if t == first:
                basis_copy.wait()
            upto = ((t - first + 1) * nkb) // (chunks + z_lag - first)
            project_range(0, done_kb, upto)
            done_kb = upto
    project_range(1, 0, nkb)

    pt = None
    for half in range(2):
        pick8 = (iota((8, nf * T), 0) - nf * half == iota((8, nf * T), 1) // T).astype(jnp.float32)
        d = nt_dot(pick8, racc[half], HIGHEST)
        pt = d if pt is None else pt + d

    def all_sum(val, a, b, a_s, a_r, b_s, b_r):
        a[me8] = val
        for p, dev in plane_peers:
            remote(a.at[me8], a.at[me8], a_s.at[p], a_r.at[me8], dev).start()
        for p, dev in plane_peers:
            remote(a.at[p], a.at[p], a_s.at[p], a_r.at[p], dev).wait_recv()
        val = a[0]
        for i in range(1, 8):
            val = val + a[i]
        b[g] = val
        for p, dev in group_peers:
            remote(b.at[g], b.at[g], b_s.at[p], b_r.at[g], dev).start()
        for p, dev in group_peers:
            remote(b.at[p], b.at[p], b_s.at[p], b_r.at[p], dev).wait_recv()
        val = b[0]
        for i in range(1, groups):
            val = val + b[i]
        return val

    def all_sum_sent(a, b, a_s, a_r, b_s, b_r):
        for p, dev in plane_peers:
            remote(a.at[me8], a.at[me8], a_s.at[p], a_r.at[me8], dev).wait_send()
        for p, dev in group_peers:
            remote(b.at[g], b.at[g], b_s.at[p], b_r.at[g], dev).wait_send()

    coeffs = all_sum(pt, pa, pb, pa_s, pa_r, pb_s, pb_r)
    coef_ref[...] = coeffs
    cb = coeffs.astype(jnp.bfloat16)

    ns = 2 * nf

    tall = jnp.broadcast_to(cb.astype(jnp.float32)[None], (nkb, ns, nk)).reshape(nkb * ns, nk)
    own = iota((nkb * ns, nk), 0) // ns == iota((nkb * ns, nk), 1) // T
    tall = jnp.where(own, tall, 0.0).astype(jnp.bfloat16)
    lanes = jnp.dot(tall, rep16[...], preferred_element_type=jnp.float32)
    keep = same_row(ns * T, T * T)
    for kb in range(nkb):
        row = lanes[kb * ns:(kb + 1) * ns, :]
        full = jnp.broadcast_to(row[:, None, :], (ns, T, T * T)).reshape(ns * T, T * T)
        cbig[kb] = jnp.where(keep, full, 0.0).astype(jnp.bfloat16)

    def residual(i, gram):
        x = i // nyg
        y0 = pl.multiple_of((i % nyg) * T, T)
        acc = None
        for kb in range(nkb):
            rhs = bas[kb * T:(kb + 1) * T, x, pl.ds(y0, T), :].reshape(T * T, nz)
            d = jnp.dot(cbig[kb], rhs, preferred_element_type=jnp.float32)
            acc = d if acc is None else acc + d
        snap = jnp.concatenate(
            [s1[:, x, pl.ds(y0, T), :].reshape(nf * T, nz), adv_ref[:, x, pl.ds(y0, T), :].reshape(nf * T, nz)],
            axis=0,
        )
        w = snap - acc
        wres[i] = w
        return gram + nt_dot(w, w, HIGHEST)

    gram = lax.fori_loop(0, cells, residual, jnp.zeros((ns * T, ns * T), jnp.float32), unroll=2)
    gram = jnp.where(same_row(ns * T, ns * T), gram, 0.0)
    gram = jnp.sum(gram.reshape(ns, T, ns * T), axis=1)
    gram = all_sum(gram, ga, gb, ga_s, ga_r, gb_s, gb_r)

    wide = ns * T
    fold = (iota((wide, wide), 0) // T == iota((wide, wide), 1)).astype(jnp.float32)
    rows, cols = iota((ns, wide), 0), iota((ns, wide), 1)
    aug = jnp.dot(gram, fold, precision=HIGHEST, preferred_element_type=jnp.float32)
    aug = jnp.where(cols == rows + ns, 1.0, aug)
    for p in range(ns):
        col = jnp.broadcast_to(aug[:, p:p + 1], (ns, wide))
        inv = 1.0 / jnp.sqrt(jnp.broadcast_to(col[p:p + 1, :], (ns, wide)))
        top = jnp.broadcast_to(aug[p:p + 1, :], (ns, wide)) * inv
        aug = jnp.where(rows == p, top, jnp.where(rows > p, aug - (col * inv) * top, aug))
    r_ref[...] = jnp.where(cols >= rows, aug, 0.0)[:, :ns]

    unfold = (iota((wide, wide), 0) == ns + iota((wide, wide), 1) // T).astype(jnp.float32)
    mix = jnp.dot(aug, unfold, precision=HIGHEST, preferred_element_type=jnp.float32)
    mix = jnp.broadcast_to(mix[:, None, :], (ns, T, wide)).reshape(wide, wide)
    mix = jnp.where(same_row(wide, wide), mix, 0.0)

    def solve(i, carry):
        x = i // nyg
        y0 = pl.multiple_of((i % nyg) * T, T)
        d = jnp.dot(mix, wres[i], precision=HIGHEST, preferred_element_type=jnp.float32)
        dir_ref[:, x, pl.ds(y0, T), :] = d.reshape(ns, T, nz)
        return carry

    lax.fori_loop(0, cells, solve, 0, unroll=4)

    for c in range(chunks):
        part_copy(c).wait_send()
        fwd_copy(c).wait_send()
    for e in range(2):
        for f in range(nf):
            y_copy(e, f).wait_send()

    @pl.when(edge_chip)
    def _():
        for c in range(chunks):
            z_copy(c).wait_send()
    all_sum_sent(pa, pb, pa_s, pa_r, pb_s, pb_r)
    all_sum_sent(ga, gb, ga_s, ga_r, gb_s, gb_r)


def on_device(velocity, basis, mean_flow, shear):
    nf, nx, ny, nz = velocity.shape
    nk = basis.shape[0]
    groups = lax.axis_size("slab") // 4
    ns = 2 * nf
    cells = nx * ny // T
    f32, bf16 = jnp.float32, jnp.bfloat16
    chunks = 2 * nf * nx
    dma = pltpu.SemaphoreType.DMA
    vmem = pl.BlockSpec(memory_space=pltpu.VMEM)
    scratch = [
        pltpu.VMEM((nf, nx, ny, nz), f32),
        pltpu.VMEM((1, mean_flow.shape[0]), f32),
        pltpu.VMEM((1, shear.shape[0]), f32),
        pltpu.VMEM((nk, T * T), bf16),
        pltpu.VMEM((nk, nx, ny, nz), bf16),
        pltpu.VMEM((nf, nx, ny, nz), f32),
        pltpu.VMEM((2, 3, nf, nx, ny, nz), f32),
        pltpu.VMEM((2, nf, nx, 8, nz), f32),
        pltpu.VMEM((nx, ny + 16, nz), f32),
        pltpu.VMEM((2, ny, nz), f32),
        pltpu.VMEM((nf, nx, ny, nz), f32),
        pltpu.VMEM((2, cells, nf * T, nz), bf16),
        pltpu.VMEM((2, nk, nf * T), f32),
        pltpu.VMEM((nk // T, ns * T, T * T), bf16),
        pltpu.VMEM((cells, ns * T, nz), f32),
        pltpu.VMEM((8, ns, nk), f32),
        pltpu.VMEM((groups, ns, nk), f32),
        pltpu.VMEM((8, ns, ns * T), f32),
        pltpu.VMEM((groups, ns, ns * T), f32),
        dma((3,)),
        dma,
        *([dma((chunks,))] * 6),
        *([dma((2 * nf,))] * 2),
        *([dma((8,))] * 2),
        *([dma((groups,))] * 2),
        *([dma((8,))] * 2),
        *([dma((groups,))] * 2),
    ]
    advanced, coeffs, rfactor, directions = pl.pallas_call(
        functools.partial(kernel, groups),
        out_shape=[
            jax.ShapeDtypeStruct((nf, nx, ny, nz), f32),
            jax.ShapeDtypeStruct((ns, nk), f32),
            jax.ShapeDtypeStruct((ns, ns), f32),
            jax.ShapeDtypeStruct((ns, nx, ny, nz), f32),
        ],
        in_specs=[pl.BlockSpec(memory_space=pl.ANY)] * 4,
        out_specs=[vmem] * 4,
        scratch_shapes=scratch,
        compiler_params=pltpu.CompilerParams(
            collective_id=0, has_side_effects=True, vmem_limit_bytes=60 * 1024 * 1024
        ),
    )(velocity, basis, mean_flow.reshape(1, -1), shear.reshape(1, -1))
    return advanced, coeffs.T, rfactor, directions


def solution(mesh):
    return jax.shard_map(
        on_device,
        mesh=mesh,
        in_specs=(P(None, "slab", "role", None), P(None, "slab", "role", None), P(), P()),
        out_specs=(P(None, "slab", "role", None), P(), P(), P(None, "slab", "role", None)),
        check_vma=False,
    )
```

```python
import functools

import jax
import jax.numpy as jnp
from jax import lax
from jax.experimental import pallas as pl
from jax.experimental.pallas import tpu as pltpu
from jax.sharding import PartitionSpec as P

viscosity = 0.1
time_step = 0.4
MESH = pl.DeviceIdType.MESH
HIGHEST = lax.Precision.HIGHEST
T = 16


def iota(shape, dim):
    return lax.broadcasted_iota(jnp.int32, shape, dim)


def same_row(rows, cols):
    return (iota((rows, cols), 0) % T) == (iota((rows, cols), 1) % T)


def nt_dot(a, b, precision=None):
    return lax.dot_general(
        a, b, (((1,), (1,)), ((), ())), precision=precision, preferred_element_type=jnp.float32
    )


def kernel(groups, v_hbm, basis_ref, flow_hbm, shear_hbm,
           adv_ref, coef_ref, r_ref, mix_ref, wres,
           v_ref, flow_ref, shear_ref, rep16,
           bas, s1, halo, yh, yx, prof, tend, sbf, racc, cbig,
           pa, pb, ga, gb,
           in_sem, bas_sem, part_s, part_r, fwd_s, fwd_r, z_s, z_r, y_s, y_r,
           pa_s, pa_r, pb_s, pb_r, ga_s, ga_r, gb_s, gb_r):
    nf, nx, ny, nz = v_ref.shape
    nk = bas.shape[0]
    nyg = ny // T
    cells = nx * nyg
    role = lax.axis_index("role")
    slab = lax.axis_index("slab")
    j = slab % 4
    g = slab // 4
    base = g * 4
    partner = base + j + 1 - 2 * (j % 2)
    across = base + (j + 2) % 4
    zto = ((g + 1 - 2 * (j // 2) + groups) % groups) * 4 + j
    lslot = (1 - j % 2) * (2 - j // 2)
    rslot = (j % 2) * (1 + j // 2)
    me8 = role * 4 + j

    small = [(v_hbm, v_ref), (flow_hbm, flow_ref), (shear_hbm, shear_ref)]
    loads = [pltpu.make_async_copy(src, dst, in_sem.at[i]) for i, (src, dst) in enumerate(small)]
    for load in loads:
        load.start()
    basis_copy = pltpu.make_async_copy(basis_ref, bas, bas_sem)
    basis_copy.start()

    barrier = pltpu.get_barrier_semaphore()
    plane_peers = []
    for o in range(1, 8):
        p = (me8 + o) % 8
        plane_peers.append((p, (p // 4, base + p % 4)))
    group_peers = []
    for o in range(1, groups):
        p = (g + o) % groups
        group_peers.append((p, (role, p * 4 + j)))
    for _, dev in plane_peers + group_peers:
        pl.semaphore_signal(barrier, inc=1, device_id=dev, device_id_type=MESH)
    for load in loads:
        load.wait()
    pl.semaphore_wait(barrier, 6 + groups)

    def remote(src, dst, ss, rs, dev):
        return pltpu.make_async_remote_copy(
            src_ref=src, dst_ref=dst, send_sem=ss, recv_sem=rs, device_id=dev, device_id_type=MESH
        )

    chunks = 2 * nf * nx
    window, fwd_lag, z_lag = 4, 2, 4

    def where_of(c):
        e, rest = divmod(c, nf * nx)
        return e, rest // nx, rest % nx

    def part_copy(c):
        e, f, x = where_of(c)
        src = (v_ref if e == 0 else s1).at[f, x]
        return remote(src, halo.at[e, 0, f, x], part_s.at[c], part_r.at[c], (role, partner))

    def fwd_copy(c):
        e, f, x = where_of(c)
        return remote(halo.at[e, 0, f, x], halo.at[e, 1, f, x], fwd_s.at[c], fwd_r.at[c], (role, across))

    def z_copy(c):
        e, f, x = where_of(c)
        return remote(halo.at[e, 1, f, x], halo.at[e, 2, f, x], z_s.at[c], z_r.at[c], (role, zto))

    row0 = pl.multiple_of((1 - role) * (ny - 8), 8)

    def y_copy(e, f):
        src = (v_ref if e == 0 else s1).at[f, :, pl.ds(row0, 8), :]
        i = e * nf + f
        return remote(src, yh.at[e, f], y_s.at[i], y_r.at[i], (1 - role, slab))

    for c in range(window):
        part_copy(c).start()
    for f in range(nf):
        y_copy(0, f).start()

    total = flow_ref.shape[1]
    pick = iota((ny, total), 1) == iota((ny, total), 0) + role * ny
    for i, ref in enumerate((flow_ref, shear_ref)):
        col = jnp.sum(jnp.where(pick, ref[...], 0.0), axis=1, keepdims=True)
        prof[i] = jnp.broadcast_to(col, (ny, nz))
    spot = iota((nk, T * T), 0) % T == iota((nk, T * T), 1) // T
    rep16[...] = spot.astype(jnp.float32).astype(jnp.bfloat16)
    role_f = role.astype(jnp.float32)

    def tendency(e, f):
        src = v_ref if e == 0 else s1
        layers = [halo[e, lslot, f, 0], halo[e, lslot, f, 1], src[f, 0], src[f, 1],
                  halo[e, rslot, f, 0], halo[e, rslot, f, 1]]
        out = []
        for x in range(nx):
            l2, l1, q, r1, r2 = layers[x:x + 5]
            edge = yh[e, f, x]
            yx[x, 0:8, :] = edge * role_f
            yx[x, 8:8 + ny, :] = q
            yx[x, 8 + ny:16 + ny, :] = edge * (1.0 - role_f)
            near = (l1 + r1) + (yx[x, 7:7 + ny, :] + yx[x, 9:9 + ny, :])
            far = (l2 + r2) + (yx[x, 6:6 + ny, :] + yx[x, 10:10 + ny, :])
            near = near + (pltpu.roll(q, 1, 1) + pltpu.roll(q, nz - 1, 1))
            far = far + (pltpu.roll(q, 2, 1) + pltpu.roll(q, nz - 2, 1))
            first = (8.0 * (r1 - l1) - (r2 - l2)) * (1.0 / 12.0)
            lap = (16.0 * near - far - 90.0 * q) * (viscosity / 12.0)
            res = lap - prof[0] * first
            if f == 0:
                res = res - prof[1] * src[1, x]
            out.append(res)
        return out

    def keep_rounded(half, f, x, vals):
        for yg in range(nyg):
            sbf[half, x * nyg + yg, f * T:(f + 1) * T, :] = vals[yg * T:(yg + 1) * T, :].astype(jnp.bfloat16)

    def project(half, kb):
        acc = None
        for i in range(cells):
            x, y0 = i // nyg, (i % nyg) * T
            lhs = bas[pl.ds(kb * T, T), x, y0:y0 + T, :].reshape(T * T, nz)
            d = nt_dot(lhs, sbf[half, i])
            acc = d if acc is None else acc + d
        acc = jnp.where(same_row(T * T, nf * T), acc, 0.0)
        racc[half, pl.ds(pl.multiple_of(kb * T, T), T), :] = jnp.sum(acc.reshape(T, T, nf * T), axis=1)

    def project_range(half, lo, hi):
        def body(kb, carry):
            project(half, kb)
            return carry
        lax.fori_loop(lo, hi, body, 0, unroll=2)

    nkb = nk // T
    edge_chip = j % 3 == 0
    done_kb = 0
    for t in range(chunks + z_lag):
        if t < chunks:
            part_copy(t).wait_recv()
            fwd_copy(t).start()
            if t + window < nf * nx:
                part_copy(t + window).start()
        if 0 <= t - fwd_lag < chunks:
            fwd_copy(t - fwd_lag).wait_recv()

            @pl.when(edge_chip)
            def _():
                z_copy(t - fwd_lag).start()
        if t - z_lag >= 0:
            c = t - z_lag

            @pl.when(edge_chip)
            def _():
                z_copy(c).wait_recv()
            e, f, x = where_of(c)
            if x == nx - 1:
                y_copy(e, f).wait_recv()
                tens = tendency(e, f)
                if e == 0:
                    for xx in range(nx):
                        val = v_ref[f, xx] + (time_step * 8.0 / 15.0) * tens[xx]
                        s1[f, xx] = val
                        tend[f, xx] = tens[xx]
                        keep_rounded(0, f, xx, val)
                    for xx in range(nx):
                        part_copy(nf * nx + f * nx + xx).start()
                    y_copy(1, f).start()
                else:
                    for xx in range(nx):
                        val = s1[f, xx] + (
                            (time_step * 5.0 / 12.0) * tens[xx] - (time_step * 17.0 / 60.0) * tend[f, xx]
                        )
                        adv_ref[f, xx] = val
                        keep_rounded(1, f, xx, val)
        first = nf * nx + z_lag
        if t >= first:
            if t == first:
                basis_copy.wait()
            upto = ((t - first + 1) * nkb) // (chunks + z_lag - first)
            project_range(0, done_kb, upto)
            done_kb = upto
    project_range(1, 0, nkb)

    pt = None
    for half in range(2):
        pick8 = (iota((8, nf * T), 0) - nf * half == iota((8, nf * T), 1) // T).astype(jnp.float32)
        d = nt_dot(pick8, racc[half], HIGHEST)
        pt = d if pt is None else pt + d

    def all_sum(val, a, b, a_s, a_r, b_s, b_r):
        a[me8] = val
        for p, dev in plane_peers:
            remote(a.at[me8], a.at[me8], a_s.at[p], a_r.at[me8], dev).start()
        for p, dev in plane_peers:
            remote(a.at[p], a.at[p], a_s.at[p], a_r.at[p], dev).wait_recv()
        val = a[0]
        for i in range(1, 8):
            val = val + a[i]
        b[g] = val
        for p, dev in group_peers:
            remote(b.at[g], b.at[g], b_s.at[p], b_r.at[g], dev).start()
        for p, dev in group_peers:
            remote(b.at[p], b.at[p], b_s.at[p], b_r.at[p], dev).wait_recv()
        val = b[0]
        for i in range(1, groups):
            val = val + b[i]
        return val

    def all_sum_sent(a, b, a_s, a_r, b_s, b_r):
        for p, dev in plane_peers:
            remote(a.at[me8], a.at[me8], a_s.at[p], a_r.at[me8], dev).wait_send()
        for p, dev in group_peers:
            remote(b.at[g], b.at[g], b_s.at[p], b_r.at[g], dev).wait_send()

    coeffs = all_sum(pt, pa, pb, pa_s, pa_r, pb_s, pb_r)
    coef_ref[...] = coeffs
    cb = coeffs.astype(jnp.bfloat16)

    ns = 2 * nf

    tall = jnp.broadcast_to(cb.astype(jnp.float32)[None], (nkb, ns, nk)).reshape(nkb * ns, nk)
    own = iota((nkb * ns, nk), 0) // ns == iota((nkb * ns, nk), 1) // T
    tall = jnp.where(own, tall, 0.0).astype(jnp.bfloat16)
    lanes = jnp.dot(tall, rep16[...], preferred_element_type=jnp.float32)
    keep = same_row(ns * T, T * T)
    for kb in range(nkb):
        row = lanes[kb * ns:(kb + 1) * ns, :]
        full = jnp.broadcast_to(row[:, None, :], (ns, T, T * T)).reshape(ns * T, T * T)
        cbig[kb] = jnp.where(keep, full, 0.0).astype(jnp.bfloat16)

    def residual(i, gram):
        x = i // nyg
        y0 = pl.multiple_of((i % nyg) * T, T)
        acc = None
        for kb in range(nkb):
            rhs = bas[kb * T:(kb + 1) * T, x, pl.ds(y0, T), :].reshape(T * T, nz)
            d = jnp.dot(cbig[kb], rhs, preferred_element_type=jnp.float32)
            acc = d if acc is None else acc + d
        snap = jnp.concatenate(
            [s1[:, x, pl.ds(y0, T), :].reshape(nf * T, nz), adv_ref[:, x, pl.ds(y0, T), :].reshape(nf * T, nz)],
            axis=0,
        )
        w = snap - acc
        wres[i] = w
        return gram + nt_dot(w, w, HIGHEST)

    gram = lax.fori_loop(0, cells, residual, jnp.zeros((ns * T, ns * T), jnp.float32), unroll=2)
    gram = jnp.where(same_row(ns * T, ns * T), gram, 0.0)
    gram = jnp.sum(gram.reshape(ns, T, ns * T), axis=1)
    gram = all_sum(gram, ga, gb, ga_s, ga_r, gb_s, gb_r)

    wide = ns * T
    fold = (iota((wide, wide), 0) // T == iota((wide, wide), 1)).astype(jnp.float32)
    rows, cols = iota((ns, wide), 0), iota((ns, wide), 1)
    aug = jnp.dot(gram, fold, precision=HIGHEST, preferred_element_type=jnp.float32)
    aug = jnp.where(cols == rows + ns, 1.0, aug)
    for p in range(ns):
        col = jnp.broadcast_to(aug[:, p:p + 1], (ns, wide))
        inv = 1.0 / jnp.sqrt(jnp.broadcast_to(col[p:p + 1, :], (ns, wide)))
        top = jnp.broadcast_to(aug[p:p + 1, :], (ns, wide)) * inv
        aug = jnp.where(rows == p, top, jnp.where(rows > p, aug - (col * inv) * top, aug))
    r_ref[...] = jnp.where(cols >= rows, aug, 0.0)[:, :ns]

    unfold = (iota((wide, wide), 0) == ns + iota((wide, wide), 1) // T).astype(jnp.float32)
    mix = jnp.dot(aug, unfold, precision=HIGHEST, preferred_element_type=jnp.float32)
    mix = jnp.broadcast_to(mix[:, None, :], (ns, T, wide)).reshape(wide, wide)
    mix_ref[...] = jnp.where(same_row(wide, wide), mix, 0.0)

    for c in range(chunks):
        part_copy(c).wait_send()
        fwd_copy(c).wait_send()
    for e in range(2):
        for f in range(nf):
            y_copy(e, f).wait_send()

    @pl.when(edge_chip)
    def _():
        for c in range(chunks):
            z_copy(c).wait_send()
    all_sum_sent(pa, pb, pa_s, pa_r, pb_s, pb_r)
    all_sum_sent(ga, gb, ga_s, ga_r, gb_s, gb_r)


def finish(adv_in, coef_in, r_in, mix_ref, wres, adv_ref, coef_ref, r_ref, dir_ref):
    ns, nx, ny, nz = dir_ref.shape
    nyg = ny // T
    adv_ref[...] = adv_in[...]
    coef_ref[...] = coef_in[...]
    r_ref[...] = r_in[...]
    for i in range(nx * nyg):
        x, y0 = i // nyg, (i % nyg) * T
        d = jnp.dot(mix_ref[...], wres[i], precision=HIGHEST, preferred_element_type=jnp.float32)
        dir_ref[:, x, y0:y0 + T, :] = d.reshape(ns, T, nz)


def on_device(velocity, basis, mean_flow, shear):
    nf, nx, ny, nz = velocity.shape
    nk = basis.shape[0]
    groups = lax.axis_size("slab") // 4
    ns = 2 * nf
    cells = nx * ny // T
    f32, bf16 = jnp.float32, jnp.bfloat16
    chunks = 2 * nf * nx
    dma = pltpu.SemaphoreType.DMA
    vmem = pl.BlockSpec(memory_space=pltpu.VMEM)
    scratch = [
        pltpu.VMEM((nf, nx, ny, nz), f32),
        pltpu.VMEM((1, mean_flow.shape[0]), f32),
        pltpu.VMEM((1, shear.shape[0]), f32),
        pltpu.VMEM((nk, T * T), bf16),
        pltpu.VMEM((nk, nx, ny, nz), bf16),
        pltpu.VMEM((nf, nx, ny, nz), f32),
        pltpu.VMEM((2, 3, nf, nx, ny, nz), f32),
        pltpu.VMEM((2, nf, nx, 8, nz), f32),
        pltpu.VMEM((nx, ny + 16, nz), f32),
        pltpu.VMEM((2, ny, nz), f32),
        pltpu.VMEM((nf, nx, ny, nz), f32),
        pltpu.VMEM((2, cells, nf * T, nz), bf16),
        pltpu.VMEM((2, nk, nf * T), f32),
        pltpu.VMEM((nk // T, ns * T, T * T), bf16),
        pltpu.VMEM((8, ns, nk), f32),
        pltpu.VMEM((groups, ns, nk), f32),
        pltpu.VMEM((8, ns, ns * T), f32),
        pltpu.VMEM((groups, ns, ns * T), f32),
        dma((3,)),
        dma,
        *([dma((chunks,))] * 6),
        *([dma((2 * nf,))] * 2),
        *([dma((8,))] * 2),
        *([dma((groups,))] * 2),
        *([dma((8,))] * 2),
        *([dma((groups,))] * 2),
    ]
    results = pl.pallas_call(
        functools.partial(kernel, groups),
        out_shape=[
            jax.ShapeDtypeStruct((nf, nx, ny, nz), f32),
            jax.ShapeDtypeStruct((ns, nk), f32),
            jax.ShapeDtypeStruct((ns, ns), f32),
            jax.ShapeDtypeStruct((ns * T, ns * T), f32),
            jax.ShapeDtypeStruct((cells, ns * T, nz), f32),
        ],
        in_specs=[pl.BlockSpec(memory_space=pl.ANY)] * 4,
        out_specs=[vmem] * 5,
        scratch_shapes=scratch,
        compiler_params=pltpu.CompilerParams(
            collective_id=0, has_side_effects=True, vmem_limit_bytes=48 * 1024 * 1024
        ),
    )(velocity, basis, mean_flow.reshape(1, -1), shear.reshape(1, -1))
    advanced, coeffs, rfactor, directions = pl.pallas_call(
        finish,
        out_shape=[
            jax.ShapeDtypeStruct((nf, nx, ny, nz), f32),
            jax.ShapeDtypeStruct((ns, nk), f32),
            jax.ShapeDtypeStruct((ns, ns), f32),
            jax.ShapeDtypeStruct((ns, nx, ny, nz), f32),
        ],
        in_specs=[vmem] * 5,
        out_specs=[vmem] * 4,
        compiler_params=pltpu.CompilerParams(vmem_limit_bytes=16 * 1024 * 1024),
    )(*results)
    return advanced, coeffs.T, rfactor, directions


def solution(mesh):
    return jax.shard_map(
        on_device,
        mesh=mesh,
        in_specs=(P(None, "slab", "role", None), P(None, "slab", "role", None), P(), P()),
        out_specs=(P(None, "slab", "role", None), P(), P(), P(None, "slab", "role", None)),
        check_vma=False,
    )
```
